32 devices in a mesh: gx: 4 (over y, x), gy: 8 (over z, core).
Axes of the slice: x: 2, y: 2, z: 4, core: 2. Of those that a mesh axis runs over, the one named last changes fastest.
Arguments:
- inv_factors: float32 [16, 32, 4096], P('gx', 'gy'), as said below
- couplings: float32 [16, 32, 2, 4096], P('gx', 'gy'), may hold values from -1.5 to 1.5
- stencil: int32 [16, 32, 2], P('gx', 'gy'), may hold values from 0 to 1
- coarse: int32 [16, 32], P('gx', 'gy'), may hold values from 0 to 1, as said below
Outputs:
- strength: float32 [16, 32, 2], P('gx', 'gy')
- restriction: bfloat16 [384, 14, 4096], P(('gx', 'gy'))
The draws below stay inside these ranges and needn't reach their ends.
Inputs may be any that keep to these rules, and one draw needn't show every extreme that they name: Each block of inv_factors is lower triangular with diagonal entries between 0.5 and 1. Each tile of 4 x 4 elements has at most 12 coarse elements, and some tile has exactly 12.
All inputs are finite; a program needn't handle non-finite values.
Results may differ from the reference program's by a relative error of at most 0.001.
Values sent between devices are 32-bit elements; how exact they have to be, the bound alone decides.
A program may use at most 64 MiB of HBM per device.

```python
import math
import jax
import jax.numpy as jnp
from jax import lax

B = 64
EX = 4
EY = 4
CAP = 12
NX = 16
NY = 32
N_GX = 4
N_GY = 8


def draw_inv_factors(key, part):
    key_diagonal, key_off = jax.random.split(key)
    full_shape = (NX, NY, B, B)
    diagonal = jnp.exp(jax.random.uniform(key_diagonal, (NX, NY, B), jnp.float32, -0.6931, 0.0))
    diagonal = jnp.clip(diagonal, 0.5, 1.0)
    off_part = jax.random.uniform(key_off, full_shape, jnp.float32, -1.0, 1.0) * (0.6 / B ** 0.5)
    identity = jnp.eye(B, dtype=jnp.float32)
    lower = jnp.tril(jnp.ones((B, B), jnp.float32), -1)
    blocks = off_part * lower + diagonal[:, :, :, None] * identity
    return blocks.reshape(NX, NY, B * B)


def draw_coarse(key, part):
    tiles_x = NX // EX
    tiles_y = NY // EY
    tile_count = tiles_x * tiles_y
    cell_count = EX * EY
    key_heavy, key_forced, key_light, key_scores = jax.random.split(key, 4)
    heavy_tile = jax.random.randint(key_heavy, (tile_count,), 0, 8) == 0
    forced = jax.random.randint(key_forced, (), 0, tile_count)
    light_count = jax.random.randint(key_light, (tile_count,), cell_count // 8, 3 * cell_count // 8 + 1)
    counts = jnp.where(heavy_tile | (jnp.arange(tile_count) == forced), CAP, light_count)
    scores = jax.random.randint(key_scores, (tile_count, cell_count), 0, 2 ** 20) * cell_count + jnp.arange(cell_count)[None, :]
    slot_rank = jnp.argsort(jnp.argsort(scores, axis=1, stable=True), axis=1, stable=True)
    coarse_flags = (slot_rank < counts[:, None]).astype(jnp.int32)
    return coarse_flags.reshape(tiles_x, tiles_y, EX, EY).transpose(0, 2, 1, 3).reshape(NX, NY)


def touch_ends(values, own_key, least, top_value):
    longest = values.shape.index(max(values.shape))
    spots = []
    for shift in (0, 1):
        where = [jax.random.randint(jax.random.fold_in(own_key, axis), (), 0, length) for axis, length in enumerate(values.shape)]
        where[longest] = (where[longest] + shift) % values.shape[longest]
        spots.append(tuple(where))
    return values.at[spots[0]].set(least).at[spots[1]].set(top_value)


def block_scale(stream_key, shape, cuts, least, largest):
    loudness, own = 1.0, jax.random.fold_in(stream_key, 6)
    for dim, blocks in cuts:
        draws = jnp.exp(jax.random.uniform(jax.random.fold_in(own, dim), (blocks,), jnp.float32, least / len(cuts), largest / len(cuts)))
        loudness = loudness * jnp.repeat(draws, shape[dim] // blocks).reshape([-1 if axis == dim else 1 for axis in range(len(shape))])
    return loudness


def gaussian(own_key, dims, scale, limit, shards=(), kind=jnp.bfloat16):
    values = scale * jax.random.normal(own_key, dims, jnp.float32)
    if shards:
        values = values * block_scale(own_key, dims, shards, -0.22, 0.18)
    return jnp.clip(values, -limit, limit).astype(kind)


def setup_inputs(seed: int = 0) -> dict:
    keys = jax.random.split(jax.random.key(seed), 5)
    return {
        "inv_factors": draw_inv_factors(jax.random.fold_in(keys[4], 71), 0),
        "couplings": gaussian(keys[1], (NX, NY, 2, B * B), 0.25, 1.5, ((0, 4), (1, 8)), jnp.float32),
        "stencil": touch_ends(jax.random.randint(keys[2], (NX, NY, 2), 0, 2), jax.random.fold_in(keys[2], 1), 0, 1).astype(jnp.int32),
        "coarse": draw_coarse(jax.random.fold_in(keys[4], 71), 0),
    }


def unfold(blocks):
    block_order = math.isqrt(blocks.shape[-1])
    return blocks.reshape(blocks.shape[:-1] + (block_order, block_order))

def fold(matrices):
    return matrices.reshape(matrices.shape[:-2] + (matrices.shape[-2] * matrices.shape[-1],))

def product(left_block, right_block):
    return fold(jnp.einsum('...ij,...jk->...ik', unfold(left_block), unfold(right_block), precision=lax.Precision.HIGHEST))

def transposed(blocks):
    return fold(jnp.swapaxes(unfold(blocks), -1, -2))

def crop_cycle(values, margin):
    return values[margin:values.shape[0] - margin, margin:values.shape[1] - margin]

def upwind_pick(values, upwind_side):
    trailing = (1,) * (values.ndim - 2)
    sign_x = upwind_side[:, :, 0].reshape(upwind_side.shape[:2] + trailing)
    sign_y = upwind_side[:, :, 1].reshape(upwind_side.shape[:2] + trailing)
    upwind_x = jnp.where(sign_x == 1, values[2:, 1:-1], values[:-2, 1:-1])
    upwind_y = jnp.where(sign_y == 1, values[1:-1, 2:], values[1:-1, :-2])
    return (upwind_x, upwind_y)

def near_paths(fine_inverse, coupling, upwind_side):
    upwind_x, upwind_y = upwind_pick(fine_inverse, crop_cycle(upwind_side, 1))
    middle = crop_cycle(fine_inverse, 1)
    local_coupling = crop_cycle(coupling, 1)
    step_x = product(-local_coupling[:, :, 0], upwind_x)
    step_y = product(-local_coupling[:, :, 1], upwind_y)
    return jnp.stack([middle, product(middle, step_x), product(middle, step_y)], axis=2)

def far_paths(fine_inverse, coupling, upwind_side, near):
    upwind_x, upwind_y = upwind_pick(near, crop_cycle(upwind_side, 2))
    middle = crop_cycle(fine_inverse, 2)
    local_coupling = crop_cycle(coupling, 2)
    lead_x = product(middle, -local_coupling[:, :, 0])[:, :, None]
    lead_y = product(middle, -local_coupling[:, :, 1])[:, :, None]
    return jnp.concatenate([middle[:, :, None], product(lead_x, upwind_x), product(lead_y, upwind_y)], axis=2)

def strength_of(factor_cycle, coupling, upwind_side):
    upwind_x, upwind_y = upwind_pick(factor_cycle, upwind_side)
    own_block = crop_cycle(factor_cycle, 1)
    result = []
    for direction, upwind_factor in ((0, upwind_x), (1, upwind_y)):
        scaled = product(product(own_block, coupling[:, :, direction]), transposed(upwind_factor))
        result.append(lax.optimization_barrier(jnp.mean(scaled * scaled, axis=-1)))
    return jnp.stack(result, axis=-1)

def restriction_rows(paths_cycle, coupling, upwind_side, coarse, capacity):
    upwind_x, upwind_y = upwind_pick(paths_cycle, upwind_side)
    cell_count = coarse.shape[0] * coarse.shape[1]
    flat_coarse = coarse.reshape(cell_count).astype(jnp.int32)
    slot_rank = jnp.cumsum(flat_coarse, dtype=jnp.int32) - flat_coarse
    chosen = ((slot_rank[None, :] == jnp.arange(capacity, dtype=jnp.int32)[:, None]) & (flat_coarse[None, :] == 1)).astype(jnp.int32)
    source = lax.optimization_barrier(jnp.sum(chosen * jnp.arange(cell_count, dtype=jnp.int32)[None, :], axis=1, dtype=jnp.int32))
    filled = lax.optimization_barrier(jnp.sum(chosen, axis=1, dtype=jnp.int32))
    rows_x = jnp.take(upwind_x.reshape((cell_count,) + upwind_x.shape[2:]), source, axis=0)
    rows_y = jnp.take(upwind_y.reshape((cell_count,) + upwind_y.shape[2:]), source, axis=0)
    coupling_rows = jnp.take(coupling.reshape((cell_count,) + coupling.shape[2:]), source, axis=0)
    restrict = jnp.concatenate([product(-coupling_rows[:, 0:1], rows_x), product(-coupling_rows[:, 1:2], rows_y)], axis=1)
    return (restrict * filled[:, None, None].astype(restrict.dtype)).astype(jnp.bfloat16)

def reference(inv_factors, couplings, stencil, coarse):
    cycle_depth = 3
    float_type = inv_factors.dtype
    pad_spec = ((cycle_depth, cycle_depth), (cycle_depth, cycle_depth))
    padded_factor = jnp.pad(inv_factors, pad_spec + ((0, 0),))
    padded_coupling = jnp.pad(couplings, pad_spec + ((0, 0), (0, 0)))
    padded_stencil = jnp.pad(stencil, pad_spec + ((0, 0),))
    padded_coarse = jnp.pad(coarse, pad_spec)
    identity_flat = jnp.eye(B, dtype=float_type).reshape(B * B)
    span_x = EX + 2 * cycle_depth
    span_y = EY + 2 * cycle_depth

    def one_tile(tile_index):
        start_x = (tile_index // N_GY * EX).astype(jnp.int32)
        start_y = (tile_index % N_GY * EY).astype(jnp.int32)
        zero_index = jnp.zeros((), jnp.int32)
        factor_inverse = lax.dynamic_slice(padded_factor, (start_x, start_y, zero_index), (span_x, span_y, B * B))
        coupling = lax.dynamic_slice(padded_coupling, (start_x, start_y, zero_index, zero_index), (span_x, span_y, 2, B * B))
        upwind_side = lax.dynamic_slice(padded_stencil, (start_x, start_y, zero_index), (span_x, span_y, 2))
        coarse_cycle = lax.dynamic_slice(padded_coarse, (start_x, start_y), (span_x, span_y))
        coord_x = start_x - cycle_depth + jnp.arange(span_x, dtype=jnp.int32)
        coord_y = start_y - cycle_depth + jnp.arange(span_y, dtype=jnp.int32)
        inside = ((coord_x >= 0) & (coord_x < NX))[:, None] & ((coord_y >= 0) & (coord_y < NY))[None, :]
        factor_inverse = jnp.where(inside[:, :, None], factor_inverse, identity_flat)
        target_x = coord_x[:, None] + 2 * upwind_side[:, :, 0] - 1
        target_y = coord_y[None, :] + 2 * upwind_side[:, :, 1] - 1
        reach = jnp.stack([(target_x >= 0) & (target_x < NX), (target_y >= 0) & (target_y < NY)], axis=-1)
        coupling = coupling * reach[:, :, :, None].astype(float_type)
        fine_inverse = (1 - coarse_cycle).astype(float_type)[:, :, None] * product(transposed(factor_inverse), factor_inverse)
        near = near_paths(fine_inverse, coupling, upwind_side)
        far = far_paths(fine_inverse, coupling, upwind_side, near)
        own_side = crop_cycle(upwind_side, cycle_depth)
        own_coupling = crop_cycle(coupling, cycle_depth)
        own_coarse = crop_cycle(coarse_cycle, cycle_depth)
        strong = strength_of(crop_cycle(factor_inverse, cycle_depth - 1), own_coupling, own_side)
        restrict = restriction_rows(far, own_coupling, own_side, own_coarse, CAP)
        return (strong, restrict)
    strong, restrict = lax.map(one_tile, jnp.arange(N_GX * N_GY, dtype=jnp.int32))
    strength = strong.reshape(N_GX, N_GY, EX, EY, 2).transpose(0, 2, 1, 3, 4).reshape(NX, NY, 2)
    return (strength, restrict.reshape(N_GX * N_GY * CAP, 14, B * B))
```

```python
import functools
import math

import jax
import jax.numpy as jnp
import numpy as np
from jax import lax
from jax.experimental import pallas as pl
from jax.experimental.pallas import tpu as pltpu
from jax.sharding import PartitionSpec as P

CAP = 12
DIRECTIONS = [(dx, dy) for dx in (-1, 0, 1) for dy in (-1, 0, 1) if (dx, dy) != (0, 0)]


def tile_of(dx, dy):
    return (dx + 1) * 3 + dy + 1


@functools.lru_cache(None)
def entries(rows_x, rows_y):
    def away(x, y):
        return max(-x, x - rows_x + 1, 0) + max(-y, y - rows_y + 1, 0)

    cells = [(x, y) for x in range(-3, rows_x + 3) for y in range(-3, rows_y + 3)]
    rings = [[c for c in cells if away(*c) == d] for d in range(4)]
    order = sum(rings, [])
    place = {c: i for i, c in enumerate(order)}
    ends = np.cumsum([len(r) for r in rings]).tolist()
    table = np.zeros((len(order), 8), np.int32)
    for i, (x, y) in enumerate(order):
        tile = tile_of(x // rows_x, y // rows_y)
        local = (x % rows_x) * rows_y + y % rows_y
        near = [place.get(c, 0) for c in ((x - 1, y), (x + 1, y), (x, y - 1), (x, y + 1))]
        table[i] = [tile, local, *near, x, y]
    return table.reshape(-1), ends


def split(a):
    high = a.astype(jnp.bfloat16)
    return high, (a - high.astype(jnp.float32)).astype(jnp.bfloat16)


def dot3(a, b):
    ah, al = split(a)
    bh, bl = split(b)
    left = jnp.concatenate([ah, ah, al], axis=1)
    right = jnp.concatenate([bh, bl, bh], axis=0)
    return jnp.dot(left, right, preferred_element_type=jnp.float32)


def dot3_tn(a):
    ah, al = split(a)
    left = jnp.concatenate([ah, ah, al], axis=0)
    right = jnp.concatenate([ah, al, ah], axis=0)
    return lax.dot_general(
        left, right, (((0,), (0,)), ((), ())), preferred_element_type=jnp.float32
    )


def dot3_nt(a, b):
    ah, al = split(a)
    bh, bl = split(b)
    left = jnp.concatenate([ah, ah, al], axis=1)
    right = jnp.concatenate([bh, bl, bh], axis=1)
    return lax.dot_general(
        left, right, (((1,), (1,)), ((), ())), preferred_element_type=jnp.float32
    )


def unfold_rows(dense):
    half = dense.shape[1] // 2
    return jnp.concatenate([dense[:, :half], dense[:, half:]], axis=0)


def spans(step, count, depth):
    if step == 0:
        return pl.ds(0, count)
    return pl.ds(count - depth, depth) if step > 0 else pl.ds(0, depth)


def loop(lo, hi, width, body):
    full = (hi - lo) // width

    def step(i, carry):
        body([lo + i * width + j for j in range(width)])
        return carry

    lax.fori_loop(0, full, step, 0)
    if lo + full * width < hi:
        body([jnp.int32(i) for i in range(lo + full * width, hi)])


def kernel(
    rows_x, rows_y, order, ends,
    table, factor_ref, coupling_ref, code_ref,
    strong_ref, out_ref,
    factors, couplings, codes, code_s, up, reach, slots,
    rows, fine, pair, lead, near, far, squares, stage,
    send_sem, recv_sem, local_sem,
):
    ax, ay = lax.axis_index("gx"), lax.axis_index("gy")
    nx, ny = lax.axis_size("gx"), lax.axis_size("gy")
    own, one, two, three = ends
    half = order // 2

    def exists(dx, dy):
        px, py = ax + dx, ay + dy
        return (px >= 0) & (px < nx) & (py >= 0) & (py < ny)

    codes[...] = jnp.zeros_like(codes)
    codes[tile_of(0, 0)] = code_ref[...]
    barrier = pltpu.get_barrier_semaphore()
    for dx, dy in DIRECTIONS:
        @pl.when(exists(dx, dy))
        def _(dx=dx, dy=dy):
            pl.semaphore_signal(
                barrier, inc=1, device_id=(ax + dx, ay + dy),
                device_id_type=pl.DeviceIdType.MESH,
            )
    wide = 1 + jnp.where(ax > 0, 1, 0) + jnp.where(ax < nx - 1, 1, 0)
    tall = 1 + jnp.where(ay > 0, 1, 0) + jnp.where(ay < ny - 1, 1, 0)
    pl.semaphore_wait(barrier, wide * tall - 1)

    def copies(dx, dy):
        diagonal = dx != 0 and dy != 0
        depth = (2, 1) if diagonal else (3, 2)
        land = tile_of(-dx, -dy)
        for kind, (src, dst) in enumerate(
            ((factor_ref, factors), (coupling_ref, couplings), (code_ref, codes))
        ):
            if kind < 2:
                where = (spans(dx, rows_x, depth[kind]), spans(dy, rows_y, depth[kind]))
                source, target = src.at[where], dst.at[(land,) + where]
            else:
                source, target = src, dst.at[land]
            yield pltpu.make_async_remote_copy(
                src_ref=source, dst_ref=target,
                send_sem=send_sem.at[land, kind], recv_sem=recv_sem.at[land, kind],
                device_id=(ax + dx, ay + dy), device_id_type=pl.DeviceIdType.MESH,
            )

    for dx, dy in sorted(DIRECTIONS, key=lambda d: (d[0] == 0, abs(d[0]) + abs(d[1]))):
        @pl.when(exists(dx, dy))
        def _(dx=dx, dy=dy):
            for copy in copies(dx, dy):
                copy.start()

    def fine_of(dense_of):
        def body(ns):
            values = []
            for n in ns:
                own_rows = unfold_rows(dense_of(n))
                values.append((n, own_rows, dot3_tn(own_rows)))
            for n, own_rows, block in values:
                rows[n] = own_rows
                fine[n] = block
        return body

    def pair_of(dense_of):
        def body(ns):
            values = []
            for n in ns:
                first, second = dense_of(n, 0), dense_of(n, 1)
                even = jnp.concatenate([first[:, :order], second[:, :order]], axis=1)
                odd = jnp.concatenate([first[:, order:], second[:, order:]], axis=1)
                values.append((n, even, odd))
            for n, even, odd in values:
                pair[n, pl.ds(0, half, 2), :] = even
                pair[n, pl.ds(1, half, 2), :] = odd
        return body

    def own_factor(n):
        return factor_ref[n // rows_y, n % rows_y]

    def own_coupling(n, d):
        return coupling_ref[n // rows_y, n % rows_y, d]

    loop(0, own, 4, fine_of(own_factor))
    loop(0, own, 2, pair_of(own_coupling))

    for dx, dy in DIRECTIONS:
        @pl.when(exists(dx, dy))
        def _(dx=dx, dy=dy):
            for copy in copies(dx, dy):
                copy.wait_send()

    for dx, dy in DIRECTIONS:
        @pl.when(exists(-dx, -dy))
        def _(dx=dx, dy=dy):
            for copy in copies(dx, dy):
                copy.wait_recv()

    to_scalars = pltpu.make_async_copy(codes, code_s, local_sem)
    to_scalars.start()
    to_scalars.wait()

    def read(n, j):
        return table[n * 8 + j]

    def code_of(n):
        return code_s[read(n, 0), 0, read(n, 1)]

    def sides(n, carry):
        code = code_of(n)
        for d, base, count in ((0, ax * rows_x, nx * rows_x), (1, ay * rows_y, ny * rows_y)):
            side = (code >> d) & 1
            aim = base + read(n, 6 + d) + 2 * side - 1
            inside = (aim >= 0) & (aim < count)
            up[2 * n + d] = jnp.where(inside, read(n, 2 + 2 * d + side), n)
            reach[2 * n + d] = jnp.where(inside, -1.0, 0.0)
        return carry

    lax.fori_loop(0, two, sides, 0)

    flags = [(code_s[tile_of(0, 0), 0, n] >> 2) & 1 for n in range(own)]
    ranks, total = [], jnp.int32(0)
    for flag in flags:
        ranks.append(jnp.where(flag == 1, total, -1))
        total = total + flag
    for s in range(CAP):
        slots[s] = sum(jnp.where(ranks[n] == s, n, 0) for n in range(own))
    def is_fine(n):
        return (1 - ((code_of(n) >> 2) & 1)).astype(jnp.float32)

    def far_factor(n):
        return factors[read(n, 0), read(n, 1) // rows_y, read(n, 1) % rows_y]

    def far_coupling(n, d):
        return couplings[read(n, 0), read(n, 1) // rows_y, read(n, 1) % rows_y, d]

    loop(own, three, 4, fine_of(far_factor))
    loop(own, two, 2, pair_of(far_coupling))

    lane = lax.broadcasted_iota(jnp.int32, (order, 2 * order), 1)

    def masked_pair(n):
        return pair[n] * jnp.where(lane < order, reach[2 * n], reach[2 * n + 1])

    def near_body(ns):
        values = []
        for n in ns:
            middle = fine[n] * is_fine(n)
            leads = dot3(middle, masked_pair(n))
            steps = [middle]
            for d in range(2):
                to = up[2 * n + d]
                steps.append(dot3(leads[:, d * order : (d + 1) * order], fine[to] * is_fine(to)))
            values.append((n, leads, jnp.concatenate(steps, axis=1)))
        for n, leads, steps in values:
            lead[n] = leads
            near[n] = steps

    loop(0, two, 4, near_body)

    def far_body(ns):
        values = []
        for n in ns:
            leads = lead[n]
            parts = [near[n][:, :order]]
            for d in range(2):
                parts.append(dot3(leads[:, d * order : (d + 1) * order], near[up[2 * n + d]]))
            values.append((n, jnp.concatenate(parts, axis=1)))
        for n, parts in values:
            far[n] = parts

    loop(0, one, 2, far_body)

    def strong_body(ns):
        values = []
        for n in ns:
            scaled = dot3(rows[n], masked_pair(n))
            for d in range(2):
                block = dot3_nt(scaled[:, d * order : (d + 1) * order], rows[up[2 * n + d]])
                values.append((2 * n + d, jnp.sum(block * block, axis=0, keepdims=True)))
        for row, value in values:
            squares[pl.ds(row, 1), :] = value

    loop(0, own, 4, strong_body)
    mean = jnp.sum(squares[...], axis=1, keepdims=True) * (1.0 / (order * order))
    strong_ref[...] = jnp.broadcast_to(mean, strong_ref.shape)

    def slot_body(s, carry):
        c = slots[s]
        filled = jnp.where(s < total, 1.0, 0.0)
        for d in range(2):
            dense = coupling_ref[c // rows_y, c % rows_y, d] * (reach[2 * c + d] * filled)
            block = dot3(unfold_rows(dense), far[up[2 * c + d]])
            for w in range(7):
                cut = block[:, w * order : (w + 1) * order]
                stage[pl.ds(7 * d + w, half, 16), :] = jnp.concatenate(
                    [cut[:half], cut[half:]], axis=1
                )
        for r in range(half):
            out_ref[s, :, r * 128 : (r + 1) * 128] = stage[r * 16 : r * 16 + 14, :].astype(
                jnp.bfloat16
            )
        return carry

    lax.fori_loop(0, CAP, slot_body, 0)


def on_device(inv_factors, couplings, stencil, coarse):
    rows_x, rows_y, flat_size = inv_factors.shape
    order = math.isqrt(flat_size)
    half = order // 2
    lanes = 2 * order
    table, ends = entries(rows_x, rows_y)
    own, one, two, three = ends
    code = (stencil[:, :, 0] + 2 * stencil[:, :, 1] + 4 * coarse).reshape(1, own)
    code = jnp.pad(code, ((0, 7), (0, 128 - own)))
    dense_factor = inv_factors.reshape(rows_x, rows_y, half, lanes)
    dense_coupling = couplings.reshape(rows_x, rows_y, 2, half, lanes)
    vmem = pl.BlockSpec(memory_space=pltpu.VMEM)
    f32 = jnp.float32
    strong, restrict = pl.pallas_call(
        functools.partial(kernel, rows_x, rows_y, order, ends),
        out_shape=(
            jax.ShapeDtypeStruct((2 * own, 128), f32),
            jax.ShapeDtypeStruct((CAP, 14, flat_size), jnp.bfloat16),
        ),
        in_specs=[pl.BlockSpec(memory_space=pltpu.SMEM), vmem, vmem, vmem],
        out_specs=(vmem, vmem),
        scratch_shapes=[
            pltpu.VMEM((9, rows_x, rows_y, half, lanes), f32),
            pltpu.VMEM((9, rows_x, rows_y, 2, half, lanes), f32),
            pltpu.VMEM((9, 8, 128), jnp.int32),
            pltpu.SMEM((9, 8, 128), jnp.int32),
            pltpu.SMEM((2 * two,), jnp.int32),
            pltpu.SMEM((2 * two,), f32),
            pltpu.SMEM((CAP,), jnp.int32),
            pltpu.VMEM((three, order, order), f32),
            pltpu.VMEM((three, order, order), f32),
            pltpu.VMEM((two, order, 2 * order), f32),
            pltpu.VMEM((two, order, 2 * order), f32),
            pltpu.VMEM((two, order, 3 * order), f32),
            pltpu.VMEM((one, order, 7 * order), f32),
            pltpu.VMEM((2 * own, order), f32),
            pltpu.VMEM((half * 16, 128), f32),
            pltpu.SemaphoreType.DMA((9, 3)),
            pltpu.SemaphoreType.DMA((9, 3)),
            pltpu.SemaphoreType.DMA,
        ],
        compiler_params=pltpu.CompilerParams(
            collective_id=0, has_side_effects=True, vmem_limit_bytes=48 * 2**20
        ),
    )(jnp.asarray(table), dense_factor, dense_coupling, code)
    return strong[:, 0].reshape(rows_x, rows_y, 2), restrict


def solution(mesh):
    placed = (P("gx", "gy", None), P("gx", "gy", None, None), P("gx", "gy", None), P("gx", "gy"))
    return jax.shard_map(
        on_device,
        mesh=mesh,
        in_specs=placed,
        out_specs=(P("gx", "gy", None), P(("gx", "gy"), None, None)),
        check_vma=False,
    )
```

```python
import functools
import math

import jax
import jax.numpy as jnp
import numpy as np
from jax import lax
from jax.experimental import pallas as pl
from jax.experimental.pallas import tpu as pltpu
from jax.sharding import PartitionSpec as P

CAP = 12
ACROSS = [(-1, 0), (1, 0)]
ALONG = [(0, -1), (0, 1)]
FACES = ACROSS + ALONG
CORNERS = [(-1, -1), (-1, 1), (1, -1), (1, 1)]
DIRECTIONS = FACES + CORNERS


def tile_of(dx, dy):
    return (dx + 1) * 3 + dy + 1


@functools.lru_cache(None)
def entries(rows_x, rows_y):
    def away(x, y):
        return max(-x, x - rows_x + 1, 0) + max(-y, y - rows_y + 1, 0)

    cells = [(x, y) for x in range(-3, rows_x + 3) for y in range(-3, rows_y + 3)]
    rings = [[c for c in cells if away(*c) == d] for d in range(4)]
    order = sum(rings, [])
    place = {c: i for i, c in enumerate(order)}
    ends = np.cumsum([len(r) for r in rings]).tolist()
    table = np.zeros((len(order), 8), np.int32)
    for i, (x, y) in enumerate(order):
        tile = tile_of(x // rows_x, y // rows_y)
        local = (x % rows_x) * rows_y + y % rows_y
        near = [place.get(c, 0) for c in ((x - 1, y), (x + 1, y), (x, y - 1), (x, y + 1))]
        table[i] = [tile, local, *near, x, y]
    return table.reshape(-1), ends


def split(a):
    high = a.astype(jnp.bfloat16).astype(jnp.float32)
    return high, a - high


def half_dtype(*parts):
    return [p.astype(jnp.bfloat16) for p in parts]


def left_of(twice, low_lanes):
    order = twice.shape[1] // 2
    high, low = split(twice)
    mixed, high = half_dtype(jnp.where(low_lanes, high, low), high)
    return jnp.concatenate([mixed, high[:, :order]], axis=1)


def right_of(block):
    high, low = half_dtype(*split(block))
    return jnp.concatenate([high, high, low], axis=0)


def dot(left, right):
    return jnp.dot(left, right, preferred_element_type=jnp.float32)


def dot3_tn(twice):
    high, low = half_dtype(*split(twice))
    order = twice.shape[1] // 2
    left = jnp.concatenate([high, high, low], axis=0)[:, :order]
    right = jnp.concatenate([high, low, high], axis=0)
    return lax.dot_general(
        left, right, (((0,), (0,)), ((), ())), preferred_element_type=jnp.float32
    )


def dot3_pair(pair, right, transposed=False):
    ah, al = half_dtype(*split(pair))
    bh, bl = half_dtype(*split(right))
    axis = 1 if transposed else 0
    dims = (((1,), (axis,)), ((), ()))
    first = lax.dot_general(
        jnp.concatenate([ah, al], axis=1), jnp.concatenate([bh, bh], axis=axis), dims,
        preferred_element_type=jnp.float32,
    )
    return first + lax.dot_general(ah, bl, dims, preferred_element_type=jnp.float32)


def turned(block):
    return pltpu.roll(block, block.shape[1] // 2, 1)


def unfold_rows(dense, low_lanes):
    other = turned(dense)
    return jnp.concatenate(
        [jnp.where(low_lanes, dense, other), jnp.where(low_lanes, other, dense)], axis=0
    )


def spans(step, count, depth):
    if step == 0:
        return pl.ds(0, count)
    return pl.ds(count - depth, depth) if step > 0 else pl.ds(0, depth)


def loop(lo, hi, width, body):
    full = (hi - lo) // width

    def step(i, carry):
        body([lo + i * width + j for j in range(width)])
        return carry

    lax.fori_loop(0, full, step, 0)
    if lo + full * width < hi:
        body([jnp.int32(i) for i in range(lo + full * width, hi)])


def kernel(
    rows_x, rows_y, order, ends,
    table, own_code, factor_ref, coupling_ref, code_ref,
    strong_ref, out_ref,
    factors, couplings, codes, code_s, up, reach, slots,
    rows, fine, pair, lead, near, far, scaled, squares, stage,
    send_sem, recv_sem, local_sem,
):
    ax, ay = lax.axis_index("gx"), lax.axis_index("gy")
    nx, ny = lax.axis_size("gx"), lax.axis_size("gy")
    own, one, two, three = ends
    half = order // 2

    def exists(dx, dy):
        px, py = ax + dx, ay + dy
        return (px >= 0) & (px < nx) & (py >= 0) & (py < ny)

    codes[...] = jnp.zeros_like(codes)
    codes[tile_of(0, 0)] = code_ref[...]
    barrier = pltpu.get_barrier_semaphore()
    for dx, dy in FACES:
        @pl.when(exists(dx, dy))
        def _(dx=dx, dy=dy):
            pl.semaphore_signal(
                barrier, inc=1, device_id=(ax + dx, ay + dy),
                device_id_type=pl.DeviceIdType.MESH,
            )
    wide = jnp.where(ax > 0, 1, 0) + jnp.where(ax < nx - 1, 1, 0)
    tall = jnp.where(ay > 0, 1, 0) + jnp.where(ay < ny - 1, 1, 0)
    pl.semaphore_wait(barrier, wide + tall)

    def copy_of(dx, dy, kind):
        diagonal = dx != 0 and dy != 0
        land = tile_of(-dx, -dy)
        dst = (codes, factors, couplings)[kind]
        if diagonal:
            src = dst.at[tile_of(-dx, 0)]
        else:
            src = (code_ref, factor_ref, coupling_ref)[kind]
        if kind == 0:
            source, target = src, dst.at[land]
        else:
            depth = (0, 2, 1)[kind] if diagonal else (0, 3, 2)[kind]
            where = (spans(dx, rows_x, depth), spans(dy, rows_y, depth))
            source, target = src.at[where], dst.at[(land,) + where]
        return pltpu.make_async_remote_copy(
            src_ref=source, dst_ref=target,
            send_sem=send_sem.at[land, kind], recv_sem=recv_sem.at[land, kind],
            device_id=(ax, ay + dy) if diagonal else (ax + dx, ay + dy),
            device_id_type=pl.DeviceIdType.MESH,
        )

    def sends(dx, dy):
        return exists(-dx, 0) & exists(0, dy) if dx != 0 and dy != 0 else exists(dx, dy)

    def each(directions, kinds, act, arriving):
        for kind in kinds:
            for dx, dy in directions:
                @pl.when(exists(-dx, -dy) if arriving else sends(dx, dy))
                def _(dx=dx, dy=dy, kind=kind):
                    act(copy_of(dx, dy, kind))

    def start(directions, kinds):
        each(directions, kinds, lambda c: c.start(), False)

    def arrived(directions, kinds):
        each(directions, kinds, lambda c: c.wait_recv(), True)

    start(ACROSS + ALONG, (0, 1, 2))

    low_half = lax.broadcasted_iota(jnp.int32, (half, 2 * order), 1) < order
    low_lanes = lax.broadcasted_iota(jnp.int32, (order, 2 * order), 1) < order

    def read(n, j):
        return table[n * 8 + j]

    def sides_of(code_at):
        def sides(n, carry):
            code = code_at(n)
            spots = ((0, ax * rows_x, nx * rows_x), (1, ay * rows_y, ny * rows_y))
            for d, base, count in spots:
                side = (code >> d) & 1
                aim = base + read(n, 6 + d) + 2 * side - 1
                inside = (aim >= 0) & (aim < count)
                up[2 * n + d] = jnp.where(inside, read(n, 2 + 2 * d + side), n)
                reach[2 * n + d] = jnp.where(inside, -1.0, 0.0)
            return carry
        return sides

    def own_code_of(n):
        return own_code[0, n]

    def far_code_of(n):
        return code_s[read(n, 0), 0, read(n, 1)]

    lax.fori_loop(0, own, sides_of(own_code_of), 0)

    flags = [(own_code[0, n] >> 2) & 1 for n in range(own)]
    ranks, total = [], jnp.int32(0)
    for flag in flags:
        ranks.append(jnp.where(flag == 1, total, -1))
        total = total + flag
    for s in range(CAP):
        slots[s] = sum(jnp.where(ranks[n] == s, n, 0) for n in range(own))

    def fine_of(dense_of, code_at):
        def body(ns):
            values = []
            for n in ns:
                twice = unfold_rows(dense_of(n), low_half)
                is_fine = (1 - ((code_at(n) >> 2) & 1)).astype(jnp.float32)
                values.append((n, twice, dot3_tn(twice) * is_fine))
            for n, twice, block in values:
                rows[n] = twice
                fine[n] = block
        return body

    def lead_of(dense_of, strong):
        def body(ns):
            values = []
            for n in ns:
                first = dense_of(n, 0) * reach[2 * n]
                second = dense_of(n, 1) * reach[2 * n + 1]
                even = jnp.where(low_half, first, turned(second))
                odd = jnp.where(low_half, turned(first), second)
                values.append((n, even, odd))
            for n, even, odd in values:
                pair[n, pl.ds(0, half, 2), :] = even
                pair[n, pl.ds(1, half, 2), :] = odd
            halves, values = values, []
            for n, even, odd in halves:
                right = right_of(pair[n])
                leads = dot(left_of(fine[n], low_lanes), right)
                if strong:
                    values.append((n, leads, dot(left_of(rows[n], low_lanes), right)))
                else:
                    values.append((n, leads, None))
            for n, leads, product in values:
                lead[n] = leads
                if product is not None:
                    scaled[n] = product
        return body

    def own_factor(n):
        return factor_ref[n // rows_y, n % rows_y]

    def own_coupling(n, d):
        return coupling_ref[n // rows_y, n % rows_y, d]

    def far_factor(n):
        return factors[read(n, 0), read(n, 1) // rows_y, read(n, 1) % rows_y]

    def far_coupling(n, d):
        return couplings[read(n, 0), read(n, 1) // rows_y, read(n, 1) % rows_y, d]

    loop(0, own, 4, fine_of(own_factor, own_code_of))
    loop(0, own, 4, lead_of(own_coupling, True))

    arrived(ACROSS, (0, 1))
    start(CORNERS, (0, 1))
    arrived(ALONG, (0, 1))
    arrived(CORNERS, (0,))
    to_scalars = pltpu.make_async_copy(codes, code_s, local_sem)
    to_scalars.start()
    to_scalars.wait()
    lax.fori_loop(own, two, sides_of(far_code_of), 0)
    arrived(CORNERS, (1,))

    loop(own, three, 4, fine_of(far_factor, far_code_of))

    arrived(ACROSS, (2,))
    start(CORNERS, (2,))
    arrived(ALONG, (2,))
    arrived(CORNERS, (2,))
    loop(own, two, 4, lead_of(far_coupling, False))

    def near_body(ns):
        values = []
        for n in ns:
            first, second = fine[up[2 * n]], fine[up[2 * n + 1]]
            right = jnp.concatenate(
                [jnp.where(low_lanes, first, 0.0), jnp.where(low_lanes, 0.0, second)], axis=0
            )
            values.append((n, fine[n], dot3_pair(lead[n], right)))
        for n, block, steps in values:
            near[n, :, : 2 * order] = steps
            near[n, :, 2 * order :] = block

    loop(0, two, 4, near_body)

    def far_body(ns):
        values = []
        for n in ns:
            leads = lead[n]
            other = turned(leads)
            first = left_of(jnp.where(low_lanes, leads, other), low_lanes)
            second = left_of(jnp.where(low_lanes, other, leads), low_lanes)
            one_x = dot(first, right_of(near[up[2 * n]]))
            one_y = dot(second, right_of(near[up[2 * n + 1]]))
            values.append((n, one_x, one_y, fine[n]))
        for n, one_x, one_y, block in values:
            far[n, :, : 2 * order] = one_x[:, : 2 * order]
            far[n, :, 2 * order : 4 * order] = jnp.where(low_lanes, one_x[:, 2 * order :], block)
            far[n, :, 4 * order :] = one_y

    loop(0, one, 4, far_body)

    def strong_body(ns):
        values = []
        for n in ns:
            first, second = rows[up[2 * n]], rows[up[2 * n + 1]]
            right = jnp.concatenate(
                [jnp.where(low_lanes, first, 0.0), jnp.where(low_lanes, 0.0, second)], axis=0
            )
            block = dot3_pair(scaled[n], right, transposed=True)
            values.append((n, jnp.sum(block * block, axis=0, keepdims=True)))
        for n, value in values:
            squares[pl.ds(n, 1), :] = value

    loop(0, own, 4, strong_body)
    lane = lax.broadcasted_iota(jnp.int32, (own, 2 * order), 1)
    means = [
        jnp.sum(jnp.where(side, squares[...], 0.0), axis=1, keepdims=True)
        for side in (lane < order, lane >= order)
    ]
    strong_ref[...] = jnp.where(lane == 0, means[0], means[1]) * (1.0 / (order * order))

    def slot_body(s, carry):
        c = slots[s]
        filled = jnp.where(s < total, 1.0, 0.0)
        blocks = []
        for d in range(2):
            dense = coupling_ref[c // rows_y, c % rows_y, d] * (reach[2 * c + d] * filled)
            left = left_of(unfold_rows(dense, low_half), low_lanes)
            blocks.append(dot(left, right_of(far[up[2 * c + d]])))
        for d, block in enumerate(blocks):
            for j, (even_w, odd_w) in enumerate(((2, 3), (1, 0), (5, 6), (4, None))):
                cut = block[:, 2 * order * j : 2 * order * (j + 1)]
                top, bottom = cut[:half], cut[half:]
                stage[pl.ds(7 * d + even_w, half, 16), :] = jnp.where(
                    low_half, top, turned(bottom)
                )
                if odd_w is not None:
                    stage[pl.ds(7 * d + odd_w, half, 16), :] = jnp.where(
                        low_half, turned(top), bottom
                    )
        for r in range(half):
            out_ref[s, :, r * 128 : (r + 1) * 128] = stage[r * 16 : r * 16 + 14, :].astype(
                jnp.bfloat16
            )
        return carry

    lax.fori_loop(0, CAP, slot_body, 0)
    each(DIRECTIONS, (0, 1, 2), lambda c: c.wait_send(), False)


def on_device(inv_factors, couplings, stencil, coarse):
    rows_x, rows_y, flat_size = inv_factors.shape
    order = math.isqrt(flat_size)
    half = order // 2
    lanes = 2 * order
    table, ends = entries(rows_x, rows_y)
    own, one, two, three = ends
    code = (stencil[:, :, 0] + 2 * stencil[:, :, 1] + 4 * coarse).reshape(1, own)
    code = jnp.pad(code, ((0, 7), (0, 128 - own)))
    dense_factor = inv_factors.reshape(rows_x, rows_y, half, lanes)
    dense_coupling = couplings.reshape(rows_x, rows_y, 2, half, lanes)
    vmem = pl.BlockSpec(memory_space=pltpu.VMEM)
    smem = pl.BlockSpec(memory_space=pltpu.SMEM)
    f32 = jnp.float32
    strong, restrict = pl.pallas_call(
        functools.partial(kernel, rows_x, rows_y, order, ends),
        out_shape=(
            jax.ShapeDtypeStruct((own, 2 * order), f32),
            jax.ShapeDtypeStruct((CAP, 14, flat_size), jnp.bfloat16),
        ),
        in_specs=[smem, smem, vmem, vmem, vmem],
        out_specs=(vmem, vmem),
        scratch_shapes=[
            pltpu.VMEM((9, rows_x, rows_y, half, lanes), f32),
            pltpu.VMEM((9, rows_x, rows_y, 2, half, lanes), f32),
            pltpu.VMEM((9, 8, 128), jnp.int32),
            pltpu.SMEM((9, 8, 128), jnp.int32),
            pltpu.SMEM((2 * two,), jnp.int32),
            pltpu.SMEM((2 * two,), f32),
            pltpu.SMEM((CAP,), jnp.int32),
            pltpu.VMEM((three, order, 2 * order), f32),
            pltpu.VMEM((three, order, 2 * order), f32),
            pltpu.VMEM((two, order, 2 * order), f32),
            pltpu.VMEM((two, order, 2 * order), f32),
            pltpu.VMEM((two, order, 4 * order), f32),
            pltpu.VMEM((one, order, 8 * order), f32),
            pltpu.VMEM((own, order, 2 * order), f32),
            pltpu.VMEM((own, 2 * order), f32),
            pltpu.VMEM((half * 16, 128), f32),
            pltpu.SemaphoreType.DMA((9, 3)),
            pltpu.SemaphoreType.DMA((9, 3)),
            pltpu.SemaphoreType.DMA,
        ],
        compiler_params=pltpu.CompilerParams(
            collective_id=0, has_side_effects=True, vmem_limit_bytes=48 * 2**20
        ),
    )(jnp.asarray(table), code, dense_factor, dense_coupling, code)
    return strong[:, :2].reshape(rows_x, rows_y, 2), restrict


def solution(mesh):
    placed = (P("gx", "gy", None), P("gx", "gy", None, None), P("gx", "gy", None), P("gx", "gy"))
    return jax.shard_map(
        on_device,
        mesh=mesh,
        in_specs=placed,
        out_specs=(P("gx", "gy", None), P(("gx", "gy"), None, None)),
        check_vma=False,
    )
```

```python
import functools
import math

import jax
import jax.numpy as jnp
import numpy as np
from jax import lax
from jax.experimental import pallas as pl
from jax.experimental.pallas import tpu as pltpu
from jax.sharding import PartitionSpec as P

CAP = 12
ACROSS = [(-1, 0), (1, 0)]
ALONG = [(0, -1), (0, 1)]
FACES = ACROSS + ALONG
CORNERS = [(-1, -1), (-1, 1), (1, -1), (1, 1)]
DIRECTIONS = FACES + CORNERS


def tile_of(dx, dy):
    return (dx + 1) * 3 + dy + 1


@functools.lru_cache(None)
def entries(rows_x, rows_y):
    def away(x, y):
        return max(-x, x - rows_x + 1, 0) + max(-y, y - rows_y + 1, 0)

    cells = [(x, y) for x in range(-3, rows_x + 3) for y in range(-3, rows_y + 3)]
    rings = [[c for c in cells if away(*c) == d] for d in range(4)]
    for ring in rings:
        ring.sort(key=lambda c: not 0 <= c[0] < rows_x)
    beside = [sum(0 <= c[0] < rows_x for c in ring) for ring in rings]
    order = sum(rings, [])
    place = {c: i for i, c in enumerate(order)}
    ends = np.cumsum([len(r) for r in rings]).tolist()
    table = np.zeros((len(order), 8), np.int32)
    for i, (x, y) in enumerate(order):
        tile = tile_of(x // rows_x, y // rows_y)
        local = (x % rows_x) * rows_y + y % rows_y
        near = [place.get(c, 0) for c in ((x - 1, y), (x + 1, y), (x, y - 1), (x, y + 1))]
        table[i] = [tile, local, *near, x, y]
    return table.reshape(-1), ends + beside[1:3]


def split(a):
    high = a.astype(jnp.bfloat16).astype(jnp.float32)
    return high, a - high


def half_dtype(*parts):
    return [p.astype(jnp.bfloat16) for p in parts]


def left_of(twice, low_lanes):
    order = twice.shape[1] // 2
    high, low = split(twice)
    mixed, high = half_dtype(jnp.where(low_lanes, high, low), high)
    return jnp.concatenate([mixed, high[:, :order]], axis=1)


def right_of(block):
    high, low = half_dtype(*split(block))
    return jnp.concatenate([high, high, low], axis=0)


def dot(left, right):
    return jnp.dot(left, right, preferred_element_type=jnp.float32)


def dot3_tn(twice):
    high, low = half_dtype(*split(twice))
    order = twice.shape[1] // 2
    left = jnp.concatenate([high, high, low], axis=0)[:, :order]
    right = jnp.concatenate([high, low, high], axis=0)
    return lax.dot_general(
        left, right, (((0,), (0,)), ((), ())), preferred_element_type=jnp.float32
    )


def dot3_pair(pair, right, transposed=False):
    ah, al = half_dtype(*split(pair))
    bh, bl = half_dtype(*split(right))
    axis = 1 if transposed else 0
    dims = (((1,), (axis,)), ((), ()))
    first = lax.dot_general(
        jnp.concatenate([ah, al], axis=1), jnp.concatenate([bh, bh], axis=axis), dims,
        preferred_element_type=jnp.float32,
    )
    return first + lax.dot_general(ah, bl, dims, preferred_element_type=jnp.float32)


def turned(block):
    return pltpu.roll(block, block.shape[1] // 2, 1)


def unfold_rows(dense, low_lanes):
    other = turned(dense)
    return jnp.concatenate(
        [jnp.where(low_lanes, dense, other), jnp.where(low_lanes, other, dense)], axis=0
    )


def spans(step, count, depth):
    if step == 0:
        return pl.ds(0, count)
    return pl.ds(count - depth, depth) if step > 0 else pl.ds(0, depth)


def loop(lo, hi, width, body):
    full = (hi - lo) // width

    def step(i, carry):
        body([lo + i * width + j for j in range(width)])
        return carry

    lax.fori_loop(0, full, step, 0)
    if lo + full * width < hi:
        body([jnp.int32(i) for i in range(lo + full * width, hi)])


def kernel(
    rows_x, rows_y, order, ends,
    table, own_code, factor_ref, coupling_ref, code_ref,
    strong_ref, out_ref,
    factors, couplings, codes, code_s, up, reach, slots,
    rows, fine, pair, lead, near, far, scaled, squares, stage,
    send_sem, recv_sem, local_sem, relay, relay_sem,
):
    ax, ay = lax.axis_index("gx"), lax.axis_index("gy")
    nx, ny = lax.axis_size("gx"), lax.axis_size("gy")
    own, one, two, three, beside_one, beside_two = ends
    half = order // 2
    relayed = nx == 4

    def exists(dx, dy):
        px, py = ax + dx, ay + dy
        return (px >= 0) & (px < nx) & (py >= 0) & (py < ny)

    codes[...] = jnp.zeros_like(codes)
    codes[tile_of(0, 0)] = code_ref[...]
    barrier = pltpu.get_barrier_semaphore()
    for dx, dy in FACES:
        @pl.when(exists(dx, dy))
        def _(dx=dx, dy=dy):
            pl.semaphore_signal(
                barrier, inc=1, device_id=(ax + dx, ay + dy),
                device_id_type=pl.DeviceIdType.MESH,
            )
    wide = jnp.where(ax > 0, 1, 0) + jnp.where(ax < nx - 1, 1, 0)
    tall = jnp.where(ay > 0, 1, 0) + jnp.where(ay < ny - 1, 1, 0)
    if relayed:
        pl.semaphore_signal(
            barrier, inc=1, device_id=(lax.rem(ax + 2, 4), ay),
            device_id_type=pl.DeviceIdType.MESH,
        )
        pl.semaphore_wait(barrier, wide + tall + 1)
    else:
        pl.semaphore_wait(barrier, wide + tall)

    def copy_of(dx, dy, kind):
        diagonal = dx != 0 and dy != 0
        land = tile_of(-dx, -dy)
        dst = (codes, factors, couplings)[kind]
        if diagonal:
            src = dst.at[tile_of(-dx, 0)]
        else:
            src = (code_ref, factor_ref, coupling_ref)[kind]
        if kind == 0:
            source, target = src, dst.at[land]
        else:
            depth = (0, 2, 1)[kind] if diagonal else (0, 3, 2)[kind]
            where = (spans(dx, rows_x, depth), spans(dy, rows_y, depth))
            source, target = src.at[where], dst.at[(land,) + where]
        return pltpu.make_async_remote_copy(
            src_ref=source, dst_ref=target,
            send_sem=send_sem.at[land, kind], recv_sem=recv_sem.at[land, kind],
            device_id=(ax, ay + dy) if diagonal else (ax + dx, ay + dy),
            device_id_type=pl.DeviceIdType.MESH,
        )

    def sends(dx, dy, kind):
        if dx != 0 and dy != 0:
            return exists(-dx, 0) & exists(0, dy)
        if relayed and kind == 2 and dx != 0:
            return exists(dx, dy) & (ax != (1 if dx > 0 else 2))
        return exists(dx, dy)

    def to_relay(dx):
        return pltpu.make_async_remote_copy(
            src_ref=coupling_ref.at[spans(dx, rows_x, 2)], dst_ref=relay,
            send_sem=relay_sem.at[0], recv_sem=relay_sem.at[1],
            device_id=(ax + 2 * dx, ay), device_id_type=pl.DeviceIdType.MESH,
        )

    def from_relay(dx):
        land = tile_of(-dx, 0)
        return pltpu.make_async_remote_copy(
            src_ref=relay, dst_ref=couplings.at[land, spans(dx, rows_x, 2)],
            send_sem=relay_sem.at[0], recv_sem=recv_sem.at[land, 2],
            device_id=(ax - dx, ay), device_id_type=pl.DeviceIdType.MESH,
        )

    def each(directions, kinds, act, arriving):
        for kind in kinds:
            for dx, dy in directions:
                @pl.when(exists(-dx, -dy) if arriving else sends(dx, dy, kind))
                def _(dx=dx, dy=dy, kind=kind):
                    act(copy_of(dx, dy, kind))

    def start(directions, kinds):
        each(directions, kinds, lambda c: c.start(), False)

    def arrived(directions, kinds):
        each(directions, kinds, lambda c: c.wait_recv(), True)

    start(FACES, (0,))
    if relayed:
        for dx in (1, -1):
            @pl.when(ax == (1 if dx > 0 else 2))
            def _(dx=dx):
                to_relay(dx).start()
    start(FACES, (1, 2))

    low_half = lax.broadcasted_iota(jnp.int32, (half, 2 * order), 1) < order
    low_lanes = lax.broadcasted_iota(jnp.int32, (order, 2 * order), 1) < order

    def read(n, j):
        return table[n * 8 + j]

    def sides_of(code_at):
        def sides(n, carry):
            code = code_at(n)
            spots = ((0, ax * rows_x, nx * rows_x), (1, ay * rows_y, ny * rows_y))
            for d, base, count in spots:
                side = (code >> d) & 1
                aim = base + read(n, 6 + d) + 2 * side - 1
                inside = (aim >= 0) & (aim < count)
                up[2 * n + d] = jnp.where(inside, read(n, 2 + 2 * d + side), n)
                reach[2 * n + d] = jnp.where(inside, -1.0, 0.0)
            return carry
        return sides

    def own_code_of(n):
        return own_code[0, n]

    def far_code_of(n):
        return code_s[read(n, 0), 0, read(n, 1)]

    lax.fori_loop(0, own, sides_of(own_code_of), 0)

    flags = [(own_code[0, n] >> 2) & 1 for n in range(own)]
    ranks, total = [], jnp.int32(0)
    for flag in flags:
        ranks.append(jnp.where(flag == 1, total, -1))
        total = total + flag
    for s in range(CAP):
        slots[s] = sum(jnp.where(ranks[n] == s, n, 0) for n in range(own))

    def fine_of(dense_of, code_at):
        def body(ns):
            values = []
            for n in ns:
                twice = unfold_rows(dense_of(n), low_half)
                is_fine = (1 - ((code_at(n) >> 2) & 1)).astype(jnp.float32)
                values.append((n, twice, dot3_tn(twice) * is_fine))
            for n, twice, block in values:
                rows[n] = twice
                fine[n] = block
        return body

    def lead_of(dense_of, strong):
        def body(ns):
            values = []
            for n in ns:
                first = dense_of(n, 0) * reach[2 * n]
                second = dense_of(n, 1) * reach[2 * n + 1]
                even = jnp.where(low_half, first, turned(second))
                odd = jnp.where(low_half, turned(first), second)
                values.append((n, even, odd))
            for n, even, odd in values:
                pair[n, pl.ds(0, half, 2), :] = even
                pair[n, pl.ds(1, half, 2), :] = odd
            halves, values = values, []
            for n, even, odd in halves:
                right = right_of(pair[n])
                leads = dot(left_of(fine[n], low_lanes), right)
                if strong:
                    values.append((n, leads, dot(left_of(rows[n], low_lanes), right)))
                else:
                    values.append((n, leads, None))
            for n, leads, product in values:
                lead[n] = leads
                if product is not None:
                    scaled[n] = product
        return body

    def own_factor(n):
        return factor_ref[n // rows_y, n % rows_y]

    def own_coupling(n, d):
        return coupling_ref[n // rows_y, n % rows_y, d]

    def far_factor(n):
        return factors[read(n, 0), read(n, 1) // rows_y, read(n, 1) % rows_y]

    def far_coupling(n, d):
        return couplings[read(n, 0), read(n, 1) // rows_y, read(n, 1) % rows_y, d]

    def beside_coupling(first, depth):
        def at(n, d):
            i = n - first
            side = i % 2
            column = (1 - side) * (rows_y - depth) + side * (depth - 1)
            return couplings[tile_of(0, -1) + 2 * side, i // 2, column, d]
        return at

    def across_coupling(first):
        def at(n, d):
            i = n - first
            side = i // rows_y
            row = (1 - side) * (rows_x - 1)
            return couplings[tile_of(-1, 0) + 6 * side, row, i % rows_y, d]
        return at

    loop(0, own, 4, fine_of(own_factor, own_code_of))
    loop(0, own, 4, lead_of(own_coupling, True))

    if relayed:
        for dx in (1, -1):
            @pl.when(ax == (3 if dx > 0 else 0))
            def _(dx=dx):
                to_relay(dx).wait_recv()
                from_relay(dx).start()
    arrived(ACROSS, (0, 1))
    start(CORNERS, (0, 1))
    arrived(ALONG, (0, 1))
    arrived(CORNERS, (0,))
    to_scalars = pltpu.make_async_copy(codes, code_s, local_sem)
    to_scalars.start()
    to_scalars.wait()
    lax.fori_loop(own, two, sides_of(far_code_of), 0)
    arrived(CORNERS, (1,))

    loop(own, three, 4, fine_of(far_factor, far_code_of))

    def near_body(ns):
        values = []
        for n in ns:
            first, second = fine[up[2 * n]], fine[up[2 * n + 1]]
            right = jnp.concatenate(
                [jnp.where(low_lanes, first, 0.0), jnp.where(low_lanes, 0.0, second)], axis=0
            )
            values.append((n, fine[n], dot3_pair(lead[n], right)))
        for n, block, steps in values:
            near[n, :, : 2 * order] = steps
            near[n, :, 2 * order :] = block

    arrived(ALONG, (2,))
    loop(own, own + beside_one, 4, lead_of(beside_coupling(own, 1), False))
    loop(one, one + beside_two, 4, lead_of(beside_coupling(one, 2), False))
    loop(0, own + beside_one, 4, near_body)
    loop(one, one + beside_two, 4, near_body)

    def strong_body(ns):
        values = []
        for n in ns:
            first, second = rows[up[2 * n]], rows[up[2 * n + 1]]
            right = jnp.concatenate(
                [jnp.where(low_lanes, first, 0.0), jnp.where(low_lanes, 0.0, second)], axis=0
            )
            block = dot3_pair(scaled[n], right, transposed=True)
            values.append((n, jnp.sum(block * block, axis=0, keepdims=True)))
        for n, value in values:
            squares[pl.ds(n, 1), :] = value

    loop(0, own, 4, strong_body)
    arrived(ACROSS, (2,))
    start(CORNERS, (2,))
    loop(own + beside_one, one, 4, lead_of(across_coupling(own + beside_one), False))
    loop(own + beside_one, one, 4, near_body)
    arrived(CORNERS, (2,))
    loop(one + beside_two, two, 4, lead_of(far_coupling, False))
    loop(one + beside_two, two, 4, near_body)

    def far_body(ns):
        values = []
        for n in ns:
            leads = lead[n]
            other = turned(leads)
            first = left_of(jnp.where(low_lanes, leads, other), low_lanes)
            second = left_of(jnp.where(low_lanes, other, leads), low_lanes)
            one_x = dot(first, right_of(near[up[2 * n]]))
            one_y = dot(second, right_of(near[up[2 * n + 1]]))
            values.append((n, one_x, one_y, fine[n]))
        for n, one_x, one_y, block in values:
            far[n, :, : 2 * order] = one_x[:, : 2 * order]
            far[n, :, 2 * order : 4 * order] = jnp.where(low_lanes, one_x[:, 2 * order :], block)
            far[n, :, 4 * order :] = one_y

    loop(0, one, 4, far_body)

    lane = lax.broadcasted_iota(jnp.int32, (own, 2 * order), 1)
    means = [
        jnp.sum(jnp.where(side, squares[...], 0.0), axis=1, keepdims=True)
        for side in (lane < order, lane >= order)
    ]
    strong_ref[...] = jnp.where(lane == 0, means[0], means[1]) * (1.0 / (order * order))

    def slot_body(slot_list):
        blocks = []
        for s in slot_list:
            c = slots[s]
            filled = jnp.where(s < total, 1.0, 0.0)
            for d in range(2):
                dense = coupling_ref[c // rows_y, c % rows_y, d] * (reach[2 * c + d] * filled)
                left = left_of(unfold_rows(dense, low_half), low_lanes)
                blocks.append(dot(left, right_of(far[up[2 * c + d]])))
        for i, block in enumerate(blocks):
            shelf, d = i // 2, i % 2
            for j, (even_w, odd_w) in enumerate(((2, 3), (1, 0), (5, 6), (4, None))):
                cut = block[:, 2 * order * j : 2 * order * (j + 1)]
                top, bottom = cut[:half], cut[half:]
                stage[shelf, pl.ds(7 * d + even_w, half, 16), :] = jnp.where(
                    low_half, top, turned(bottom)
                )
                if odd_w is not None:
                    stage[shelf, pl.ds(7 * d + odd_w, half, 16), :] = jnp.where(
                        low_half, turned(top), bottom
                    )
        for shelf, s in enumerate(slot_list):
            for r in range(half):
                out_ref[s, :, r * 128 : (r + 1) * 128] = stage[
                    shelf, r * 16 : r * 16 + 14, :
                ].astype(jnp.bfloat16)

    loop(0, CAP, 2, slot_body)
    each(DIRECTIONS, (0, 1, 2), lambda c: c.wait_send(), False)
    if relayed:
        for dx in (1, -1):
            @pl.when((ax == (1 if dx > 0 else 2)) | (ax == (3 if dx > 0 else 0)))
            def _(dx=dx):
                to_relay(dx).wait_send()


def on_device(inv_factors, couplings, stencil, coarse):
    rows_x, rows_y, flat_size = inv_factors.shape
    order = math.isqrt(flat_size)
    half = order // 2
    lanes = 2 * order
    table, ends = entries(rows_x, rows_y)
    own, one, two, three = ends[:4]
    code = (stencil[:, :, 0] + 2 * stencil[:, :, 1] + 4 * coarse).reshape(1, own)
    code = jnp.pad(code, ((0, 7), (0, 128 - own)))
    dense_factor = inv_factors.reshape(rows_x, rows_y, half, lanes)
    dense_coupling = couplings.reshape(rows_x, rows_y, 2, half, lanes)
    vmem = pl.BlockSpec(memory_space=pltpu.VMEM)
    smem = pl.BlockSpec(memory_space=pltpu.SMEM)
    f32 = jnp.float32
    strong, restrict = pl.pallas_call(
        functools.partial(kernel, rows_x, rows_y, order, ends),
        out_shape=(
            jax.ShapeDtypeStruct((own, 2 * order), f32),
            jax.ShapeDtypeStruct((CAP, 14, flat_size), jnp.bfloat16),
        ),
        in_specs=[smem, smem, vmem, vmem, vmem],
        out_specs=(vmem, vmem),
        scratch_shapes=[
            pltpu.VMEM((9, rows_x, rows_y, half, lanes), f32),
            pltpu.VMEM((9, rows_x, rows_y, 2, half, lanes), f32),
            pltpu.VMEM((9, 8, 128), jnp.int32),
            pltpu.SMEM((9, 8, 128), jnp.int32),
            pltpu.SMEM((2 * two,), jnp.int32),
            pltpu.SMEM((2 * two,), f32),
            pltpu.SMEM((CAP,), jnp.int32),
            pltpu.VMEM((three, order, 2 * order), f32),
            pltpu.VMEM((three, order, 2 * order), f32),
            pltpu.VMEM((two, order, 2 * order), f32),
            pltpu.VMEM((two, order, 2 * order), f32),
            pltpu.VMEM((two, order, 4 * order), f32),
            pltpu.VMEM((one, order, 8 * order), f32),
            pltpu.VMEM((own, order, 2 * order), f32),
            pltpu.VMEM((own, 2 * order), f32),
            pltpu.VMEM((2, half * 16, 128), f32),
            pltpu.SemaphoreType.DMA((9, 3)),
            pltpu.SemaphoreType.DMA((9, 3)),
            pltpu.SemaphoreType.DMA,
            pltpu.VMEM((2, rows_y, 2, half, lanes), f32),
            pltpu.SemaphoreType.DMA((2,)),
        ],
        compiler_params=pltpu.CompilerParams(
            collective_id=0, has_side_effects=True, vmem_limit_bytes=48 * 2**20
        ),
    )(jnp.asarray(table), code, dense_factor, dense_coupling, code)
    return strong[:, :2].reshape(rows_x, rows_y, 2), restrict


def solution(mesh):
    placed = (P("gx", "gy", None), P("gx", "gy", None, None), P("gx", "gy", None), P("gx", "gy"))
    return jax.shard_map(
        on_device,
        mesh=mesh,
        in_specs=placed,
        out_specs=(P("gx", "gy", None), P(("gx", "gy"), None, None)),
        check_vma=False,
    )
```

```python
import functools
import math

import jax
import jax.numpy as jnp
import numpy as np
from jax import lax
from jax.experimental import pallas as pl
from jax.experimental.pallas import tpu as pltpu
from jax.sharding import PartitionSpec as P

CAP = 12
ACROSS = [(-1, 0), (1, 0)]
ALONG = [(0, -1), (0, 1)]
FACES = ACROSS + ALONG
CORNERS = [(-1, -1), (-1, 1), (1, -1), (1, 1)]
DIRECTIONS = FACES + CORNERS


def tile_of(dx, dy):
    return (dx + 1) * 3 + dy + 1


@functools.lru_cache(None)
def entries(rows_x, rows_y):
    def away(x, y):
        return max(-x, x - rows_x + 1, 0) + max(-y, y - rows_y + 1, 0)

    cells = [(x, y) for x in range(-3, rows_x + 3) for y in range(-3, rows_y + 3)]
    rings = [[c for c in cells if away(*c) == d] for d in range(4)]
    for ring in rings:
        ring.sort(key=lambda c: not 0 <= c[0] < rows_x)
    beside = [sum(0 <= c[0] < rows_x for c in ring) for ring in rings]
    order = sum(rings, [])
    place = {c: i for i, c in enumerate(order)}
    ends = np.cumsum([len(r) for r in rings]).tolist()
    table = np.zeros((len(order), 8), np.int32)
    for i, (x, y) in enumerate(order):
        tile = tile_of(x // rows_x, y // rows_y)
        local = (x % rows_x) * rows_y + y % rows_y
        near = [place.get(c, 0) for c in ((x - 1, y), (x + 1, y), (x, y - 1), (x, y + 1))]
        table[i] = [tile, local, *near, x, y]
    return table.reshape(-1), ends + beside[1:3]


def split(a):
    high = a.astype(jnp.bfloat16).astype(jnp.float32)
    return high, a - high


def half_dtype(*parts):
    return [p.astype(jnp.bfloat16) for p in parts]


def left_of(twice, low_lanes):
    order = twice.shape[1] // 2
    high, low = split(twice)
    mixed, high = half_dtype(jnp.where(low_lanes, high, low), high)
    return jnp.concatenate([mixed, high[:, :order]], axis=1)


def right_of(block):
    high, low = half_dtype(*split(block))
    return jnp.concatenate([high, high, low], axis=0)


def dot(left, right):
    return jnp.dot(left, right, preferred_element_type=jnp.float32)


def dot3_tn(twice):
    high, low = half_dtype(*split(twice))
    order = twice.shape[1] // 2
    left = jnp.concatenate([high, high, low], axis=0)[:, :order]
    right = jnp.concatenate([high, low, high], axis=0)
    return lax.dot_general(
        left, right, (((0,), (0,)), ((), ())), preferred_element_type=jnp.float32
    )


def dot3_pair(pair, right, transposed=False):
    ah, al = half_dtype(*split(pair))
    bh, bl = half_dtype(*split(right))
    axis = 1 if transposed else 0
    dims = (((1,), (axis,)), ((), ()))
    first = lax.dot_general(
        jnp.concatenate([ah, al], axis=1), jnp.concatenate([bh, bh], axis=axis), dims,
        preferred_element_type=jnp.float32,
    )
    return first + lax.dot_general(ah, bl, dims, preferred_element_type=jnp.float32)


def turned(block):
    return pltpu.roll(block, block.shape[1] // 2, 1)


def unfold_rows(dense, low_lanes):
    other = turned(dense)
    return jnp.concatenate(
        [jnp.where(low_lanes, dense, other), jnp.where(low_lanes, other, dense)], axis=0
    )


def spans(step, count, depth):
    if step == 0:
        return pl.ds(0, count)
    return pl.ds(count - depth, depth) if step > 0 else pl.ds(0, depth)


def loop(lo, hi, width, body):
    full = (hi - lo) // width

    def step(i, carry):
        body([lo + i * width + j for j in range(width)])
        return carry

    lax.fori_loop(0, full, step, 0)
    if lo + full * width < hi:
        body([jnp.int32(i) for i in range(lo + full * width, hi)])


def kernel(
    rows_x, rows_y, order, ends,
    table, own_code, factor_ref, coupling_ref, code_ref,
    strong_ref, out_ref,
    factors, couplings, codes, code_s, up, reach, slots,
    rows, fine, pair, lead, near, far, scaled, squares, stage,
    send_sem, recv_sem, local_sem, relay, relay_sem,
):
    ax, ay = lax.axis_index("gx"), lax.axis_index("gy")
    nx, ny = lax.axis_size("gx"), lax.axis_size("gy")
    own, one, two, three, beside_one, beside_two = ends
    half = order // 2
    relayed = nx == 4

    def exists(dx, dy):
        px, py = ax + dx, ay + dy
        return (px >= 0) & (px < nx) & (py >= 0) & (py < ny)

    codes[...] = jnp.zeros_like(codes)
    codes[tile_of(0, 0)] = code_ref[...]
    barrier = pltpu.get_barrier_semaphore()
    for dx, dy in FACES:
        @pl.when(exists(dx, dy))
        def _(dx=dx, dy=dy):
            pl.semaphore_signal(
                barrier, inc=1, device_id=(ax + dx, ay + dy),
                device_id_type=pl.DeviceIdType.MESH,
            )
    wide = jnp.where(ax > 0, 1, 0) + jnp.where(ax < nx - 1, 1, 0)
    tall = jnp.where(ay > 0, 1, 0) + jnp.where(ay < ny - 1, 1, 0)
    if relayed:
        pl.semaphore_signal(
            barrier, inc=1, device_id=(lax.rem(ax + 2, 4), ay),
            device_id_type=pl.DeviceIdType.MESH,
        )
        pl.semaphore_wait(barrier, wide + tall + 1)
    else:
        pl.semaphore_wait(barrier, wide + tall)

    def copy_of(dx, dy, kind):
        diagonal = dx != 0 and dy != 0
        land = tile_of(-dx, -dy)
        dst = (codes, factors, couplings)[kind]
        if diagonal:
            src = dst.at[tile_of(-dx, 0)]
        else:
            src = (code_ref, factor_ref, coupling_ref)[kind]
        if kind == 0:
            source, target = src, dst.at[land]
        else:
            depth = (0, 2, 1)[kind] if diagonal else (0, 3, 2)[kind]
            where = (spans(dx, rows_x, depth), spans(dy, rows_y, depth))
            source, target = src.at[where], dst.at[(land,) + where]
        return pltpu.make_async_remote_copy(
            src_ref=source, dst_ref=target,
            send_sem=send_sem.at[land, kind], recv_sem=recv_sem.at[land, kind],
            device_id=(ax, ay + dy) if diagonal else (ax + dx, ay + dy),
            device_id_type=pl.DeviceIdType.MESH,
        )

    def sends(dx, dy, kind):
        if dx != 0 and dy != 0:
            return exists(-dx, 0) & exists(0, dy)
        if relayed and kind == 2 and dx != 0:
            return exists(dx, dy) & (ax != (1 if dx > 0 else 2))
        return exists(dx, dy)

    def to_relay(dx):
        return pltpu.make_async_remote_copy(
            src_ref=coupling_ref.at[spans(dx, rows_x, 2)], dst_ref=relay,
            send_sem=relay_sem.at[0], recv_sem=relay_sem.at[1],
            device_id=(ax + 2 * dx, ay), device_id_type=pl.DeviceIdType.MESH,
        )

    def from_relay(dx):
        land = tile_of(-dx, 0)
        return pltpu.make_async_remote_copy(
            src_ref=relay, dst_ref=couplings.at[land, spans(dx, rows_x, 2)],
            send_sem=relay_sem.at[0], recv_sem=recv_sem.at[land, 2],
            device_id=(ax - dx, ay), device_id_type=pl.DeviceIdType.MESH,
        )

    def each(directions, kinds, act, arriving):
        for kind in kinds:
            for dx, dy in directions:
                @pl.when(exists(-dx, -dy) if arriving else sends(dx, dy, kind))
                def _(dx=dx, dy=dy, kind=kind):
                    act(copy_of(dx, dy, kind))

    def start(directions, kinds):
        each(directions, kinds, lambda c: c.start(), False)

    def arrived(directions, kinds):
        each(directions, kinds, lambda c: c.wait_recv(), True)

    start(FACES, (0,))
    if relayed:
        for dx in (1, -1):
            @pl.when(ax == (1 if dx > 0 else 2))
            def _(dx=dx):
                to_relay(dx).start()
    start(FACES, (1,))
    start(ALONG, (2,))

    low_half = lax.broadcasted_iota(jnp.int32, (half, 2 * order), 1) < order
    low_lanes = lax.broadcasted_iota(jnp.int32, (order, 2 * order), 1) < order

    def read(n, j):
        return table[n * 8 + j]

    def sides_of(code_at):
        def sides(n, carry):
            code = code_at(n)
            spots = ((0, ax * rows_x, nx * rows_x), (1, ay * rows_y, ny * rows_y))
            for d, base, count in spots:
                side = (code >> d) & 1
                aim = base + read(n, 6 + d) + 2 * side - 1
                inside = (aim >= 0) & (aim < count)
                up[2 * n + d] = jnp.where(inside, read(n, 2 + 2 * d + side), n)
                reach[2 * n + d] = jnp.where(inside, -1.0, 0.0)
            return carry
        return sides

    def own_code_of(n):
        return own_code[0, n]

    def far_code_of(n):
        return code_s[read(n, 0), 0, read(n, 1)]

    lax.fori_loop(0, own, sides_of(own_code_of), 0)

    flags = [(own_code[0, n] >> 2) & 1 for n in range(own)]
    ranks, total = [], jnp.int32(0)
    for flag in flags:
        ranks.append(jnp.where(flag == 1, total, -1))
        total = total + flag
    for s in range(CAP):
        slots[s] = sum(jnp.where(ranks[n] == s, n, 0) for n in range(own))

    def fine_of(dense_of, code_at):
        def body(ns):
            values = []
            for n in ns:
                twice = unfold_rows(dense_of(n), low_half)
                is_fine = (1 - ((code_at(n) >> 2) & 1)).astype(jnp.float32)
                values.append((n, twice, dot3_tn(twice) * is_fine))
            for n, twice, block in values:
                rows[n] = twice
                fine[n] = block
        return body

    def lead_of(dense_of, strong):
        def body(ns):
            values = []
            for n in ns:
                first = dense_of(n, 0) * reach[2 * n]
                second = dense_of(n, 1) * reach[2 * n + 1]
                even = jnp.where(low_half, first, turned(second))
                odd = jnp.where(low_half, turned(first), second)
                values.append((n, even, odd))
            for n, even, odd in values:
                pair[n, pl.ds(0, half, 2), :] = even
                pair[n, pl.ds(1, half, 2), :] = odd
            halves, values = values, []
            for n, even, odd in halves:
                right = right_of(pair[n])
                leads = dot(left_of(fine[n], low_lanes), right)
                if strong:
                    values.append((n, leads, dot(left_of(rows[n], low_lanes), right)))
                else:
                    values.append((n, leads, None))
            for n, leads, product in values:
                lead[n] = leads
                if product is not None:
                    scaled[n] = product
        return body

    def own_factor(n):
        return factor_ref[n // rows_y, n % rows_y]

    def own_coupling(n, d):
        return coupling_ref[n // rows_y, n % rows_y, d]

    def far_factor(n):
        return factors[read(n, 0), read(n, 1) // rows_y, read(n, 1) % rows_y]

    def far_coupling(n, d):
        return couplings[read(n, 0), read(n, 1) // rows_y, read(n, 1) % rows_y, d]

    def beside_coupling(first, depth):
        def at(n, d):
            i = n - first
            side = i % 2
            column = (1 - side) * (rows_y - depth) + side * (depth - 1)
            return couplings[tile_of(0, -1) + 2 * side, i // 2, column, d]
        return at

    def across_coupling(first):
        def at(n, d):
            i = n - first
            side = i // rows_y
            row = (1 - side) * (rows_x - 1)
            return couplings[tile_of(-1, 0) + 6 * side, row, i % rows_y, d]
        return at

    loop(0, own, 4, fine_of(own_factor, own_code_of))
    loop(0, own, 4, lead_of(own_coupling, True))

    each(ACROSS, (1,), lambda c: c.wait_send(), False)
    start(ACROSS, (2,))
    if relayed:
        for dx in (1, -1):
            @pl.when(ax == (3 if dx > 0 else 0))
            def _(dx=dx):
                to_relay(dx).wait_recv()
                from_relay(dx).start()
    arrived(ACROSS, (0, 1))
    start(CORNERS, (0, 1))
    arrived(ALONG, (0, 1))
    arrived(CORNERS, (0,))
    to_scalars = pltpu.make_async_copy(codes, code_s, local_sem)
    to_scalars.start()
    to_scalars.wait()
    lax.fori_loop(own, two, sides_of(far_code_of), 0)
    arrived(CORNERS, (1,))

    loop(own, three, 4, fine_of(far_factor, far_code_of))

    def near_body(ns):
        values = []
        for n in ns:
            first, second = fine[up[2 * n]], fine[up[2 * n + 1]]
            right = jnp.concatenate(
                [jnp.where(low_lanes, first, 0.0), jnp.where(low_lanes, 0.0, second)], axis=0
            )
            values.append((n, fine[n], dot3_pair(lead[n], right)))
        for n, block, steps in values:
            near[n, :, : 2 * order] = steps
            near[n, :, 2 * order :] = block

    arrived(ALONG, (2,))
    loop(own, own + beside_one, 4, lead_of(beside_coupling(own, 1), False))
    loop(one, one + beside_two, 4, lead_of(beside_coupling(one, 2), False))
    loop(0, own + beside_one, 4, near_body)
    loop(one, one + beside_two, 4, near_body)

    def strong_body(ns):
        values = []
        for n in ns:
            first, second = rows[up[2 * n]], rows[up[2 * n + 1]]
            right = jnp.concatenate(
                [jnp.where(low_lanes, first, 0.0), jnp.where(low_lanes, 0.0, second)], axis=0
            )
            block = dot3_pair(scaled[n], right, transposed=True)
            values.append((n, jnp.sum(block * block, axis=0, keepdims=True)))
        for n, value in values:
            squares[pl.ds(n, 1), :] = value

    loop(0, own, 4, strong_body)
    arrived(ACROSS, (2,))
    start(CORNERS, (2,))
    loop(own + beside_one, one, 4, lead_of(across_coupling(own + beside_one), False))
    loop(own + beside_one, one, 4, near_body)
    arrived(CORNERS, (2,))
    loop(one + beside_two, two, 4, lead_of(far_coupling, False))
    loop(one + beside_two, two, 4, near_body)

    def far_body(ns):
        values = []
        for n in ns:
            leads = lead[n]
            other = turned(leads)
            first = left_of(jnp.where(low_lanes, leads, other), low_lanes)
            second = left_of(jnp.where(low_lanes, other, leads), low_lanes)
            one_x = dot(first, right_of(near[up[2 * n]]))
            one_y = dot(second, right_of(near[up[2 * n + 1]]))
            values.append((n, one_x, one_y, fine[n]))
        for n, one_x, one_y, block in values:
            far[n, :, : 2 * order] = one_x[:, : 2 * order]
            far[n, :, 2 * order : 4 * order] = jnp.where(low_lanes, one_x[:, 2 * order :], block)
            far[n, :, 4 * order :] = one_y

    loop(0, one, 4, far_body)

    lane = lax.broadcasted_iota(jnp.int32, (own, 2 * order), 1)
    means = [
        jnp.sum(jnp.where(side, squares[...], 0.0), axis=1, keepdims=True)
        for side in (lane < order, lane >= order)
    ]
    strong_ref[...] = jnp.where(lane == 0, means[0], means[1]) * (1.0 / (order * order))

    def slot_body(slot_list):
        blocks = []
        for s in slot_list:
            c = slots[s]
            filled = jnp.where(s < total, 1.0, 0.0)
            for d in range(2):
                dense = coupling_ref[c // rows_y, c % rows_y, d] * (reach[2 * c + d] * filled)
                left = left_of(unfold_rows(dense, low_half), low_lanes)
                blocks.append(dot(left, right_of(far[up[2 * c + d]])))
        for i, block in enumerate(blocks):
            shelf, d = i // 2, i % 2
            for j, (even_w, odd_w) in enumerate(((2, 3), (1, 0), (5, 6), (4, None))):
                cut = block[:, 2 * order * j : 2 * order * (j + 1)]
                top, bottom = cut[:half], cut[half:]
                stage[shelf, pl.ds(7 * d + even_w, half, 16), :] = jnp.where(
                    low_half, top, turned(bottom)
                )
                if odd_w is not None:
                    stage[shelf, pl.ds(7 * d + odd_w, half, 16), :] = jnp.where(
                        low_half, turned(top), bottom
                    )
        for shelf, s in enumerate(slot_list):
            for r in range(half):
                out_ref[s, :, r * 128 : (r + 1) * 128] = stage[
                    shelf, r * 16 : r * 16 + 14, :
                ].astype(jnp.bfloat16)

    loop(0, CAP, 2, slot_body)
    each(DIRECTIONS, (0, 2), lambda c: c.wait_send(), False)
    each(ALONG + CORNERS, (1,), lambda c: c.wait_send(), False)
    if relayed:
        for dx in (1, -1):
            @pl.when((ax == (1 if dx > 0 else 2)) | (ax == (3 if dx > 0 else 0)))
            def _(dx=dx):
                to_relay(dx).wait_send()


def on_device(inv_factors, couplings, stencil, coarse):
    rows_x, rows_y, flat_size = inv_factors.shape
    order = math.isqrt(flat_size)
    half = order // 2
    lanes = 2 * order
    table, ends = entries(rows_x, rows_y)
    own, one, two, three = ends[:4]
    code = (stencil[:, :, 0] + 2 * stencil[:, :, 1] + 4 * coarse).reshape(1, own)
    code = jnp.pad(code, ((0, 7), (0, 128 - own)))
    dense_factor = inv_factors.reshape(rows_x, rows_y, half, lanes)
    dense_coupling = couplings.reshape(rows_x, rows_y, 2, half, lanes)
    vmem = pl.BlockSpec(memory_space=pltpu.VMEM)
    smem = pl.BlockSpec(memory_space=pltpu.SMEM)
    f32 = jnp.float32
    strong, restrict = pl.pallas_call(
        functools.partial(kernel, rows_x, rows_y, order, ends),
        out_shape=(
            jax.ShapeDtypeStruct((own, 2 * order), f32),
            jax.ShapeDtypeStruct((CAP, 14, flat_size), jnp.bfloat16),
        ),
        in_specs=[smem, smem, vmem, vmem, vmem],
        out_specs=(vmem, vmem),
        scratch_shapes=[
            pltpu.VMEM((9, rows_x, rows_y, half, lanes), f32),
            pltpu.VMEM((9, rows_x, rows_y, 2, half, lanes), f32),
            pltpu.VMEM((9, 8, 128), jnp.int32),
            pltpu.SMEM((9, 8, 128), jnp.int32),
            pltpu.SMEM((2 * two,), jnp.int32),
            pltpu.SMEM((2 * two,), f32),
            pltpu.SMEM((CAP,), jnp.int32),
            pltpu.VMEM((three, order, 2 * order), f32),
            pltpu.VMEM((three, order, 2 * order), f32),
            pltpu.VMEM((two, order, 2 * order), f32),
            pltpu.VMEM((two, order, 2 * order), f32),
            pltpu.VMEM((two, order, 4 * order), f32),
            pltpu.VMEM((one, order, 8 * order), f32),
            pltpu.VMEM((own, order, 2 * order), f32),
            pltpu.VMEM((own, 2 * order), f32),
            pltpu.VMEM((2, half * 16, 128), f32),
            pltpu.SemaphoreType.DMA((9, 3)),
            pltpu.SemaphoreType.DMA((9, 3)),
            pltpu.SemaphoreType.DMA,
            pltpu.VMEM((2, rows_y, 2, half, lanes), f32),
            pltpu.SemaphoreType.DMA((2,)),
        ],
        compiler_params=pltpu.CompilerParams(
            collective_id=0, has_side_effects=True, vmem_limit_bytes=48 * 2**20
        ),
    )(jnp.asarray(table), code, dense_factor, dense_coupling, code)
    return strong[:, :2].reshape(rows_x, rows_y, 2), restrict


def solution(mesh):
    placed = (P("gx", "gy", None), P("gx", "gy", None, None), P("gx", "gy", None), P("gx", "gy"))
    return jax.shard_map(
        on_device,
        mesh=mesh,
        in_specs=placed,
        out_specs=(P("gx", "gy", None), P(("gx", "gy"), None, None)),
        check_vma=False,
    )
```
